32 devices in a mesh: blk: 16 (over z, y, core), mpo: 2 (over x).
Axes of the slice: x: 2, y: 2, z: 4, core: 2. Of those that a mesh axis runs over, the one named last changes fastest.
Arguments:
- wave: bfloat16 [1536, 128, 128], P('blk'), may hold values from -6 to 6
- left_env: bfloat16 [2, 64, 128, 128], P('mpo', 'blk'), may hold values from -0.5 to 0.5
- right_env: bfloat16 [2, 64, 128, 128], P('mpo', 'blk'), may hold values from -0.375 to 0.375
- right_sector: int32 [1536, 1], P('blk'), may hold values from 0 to 63; in each aligned block of 96 rows (0 to 95, 96 to 191, ...) at most 2 rows name the same one
- right_home: int32 [64], replicated, may hold values from 0 to 63, each once
Outputs:
- product: bfloat16 [1536, 128, 128], P('blk', None, 'mpo')
The draws below stay inside these ranges and needn't reach their ends.
Inputs may be any that keep to these rules, and one draw needn't show every extreme that they name: `right_sector`: among the 96 blocks of one device (aligned blocks of rows) no right sector appears more than 2 times, and some sector appears exactly 2 times; every sector appears somewhere. `right_home`: each sector has its own storage row.
All inputs are finite; a program needn't handle non-finite values.
Results may differ from the reference program's by a relative error of at most 0.008.
Values may be sent and summed in bfloat16 or wider, within the bound.
A program may use at most 64 MiB of HBM per device.

```python
import math
import jax
import jax.numpy as jnp
import numpy as np
from jax import lax

BS = 128
KL = 64
CAP = 2
BLK_DEV = 96
NB = 1536
W = 2


def shard_levels(key, dims, shards, least, largest):
    gain = 1.0
    for dim, shards_of in shards:
        heights = jax.random.uniform(jax.random.fold_in(jax.random.fold_in(key, 6), dim), (shards_of,), jnp.float32, least / len(shards), largest / len(shards))
        gain = gain * jnp.repeat(jnp.exp(heights), dims[dim] // shards_of).reshape((-1,) + (1,) * (len(dims) - 1 - dim))
    return gain


def assign_block(own_key, own, number, rows, count, top, bound, slope):
    sequence = jax.random.permutation(own_key, count)
    heavy_load, usual = shares(count, rows * top, bound, slope, True), shares(count, rows * top, bound, slope, False)
    places = jnp.arange(count)

    def named(sizes, rotation):
        used = int((sizes > 0).sum())
        fixed = max(1, used // 4)
        moved = fixed + (places - fixed + rotation * (used - fixed)) % max(1, count - fixed)
        return jnp.zeros((count,), jnp.int32).at[sequence[jnp.where(places < fixed, places, moved)]].set(jnp.asarray(sizes, jnp.int32))

    sizes = jnp.where(number % 4 == 0, named(heavy_load, number // 4), named(usual, number - number // 4 - 1))
    mixed = jax.random.permutation(jax.random.fold_in(own, 3), count)
    source_of, taker = mixed[0:count // 2 * 2:2], mixed[1:count // 2 * 2:2]
    slack = jnp.minimum(sizes[source_of] - 1, bound - sizes[taker]) // 2
    slack = jnp.where((source_of == sequence[0]) | (taker == sequence[0]) | (sizes[taker] == 0), 0, jnp.maximum(slack, 0))
    moved = jax.random.randint(jax.random.fold_in(own, 4), (count // 2,), 0, 1 << 20) % (slack + 1)
    sizes = sizes.at[source_of].add(-moved).at[taker].add(moved)
    members = jnp.searchsorted(jnp.cumsum(sizes), jnp.arange(rows * top), side="right").astype(jnp.int32)
    listing = members.reshape(top, rows).T
    listing = listing[jax.random.permutation(jax.random.fold_in(own, 1), rows)]
    rotation = jax.random.randint(jax.random.fold_in(own, 2), (rows, 1), 0, top)
    return jnp.take_along_axis(listing, (jnp.arange(top)[None, :] + rotation) % top, axis=1)


def shares(count, total, most, skew, full):
    weights = [(1 << 20) // math.isqrt(grade ** skew) + 1 for grade in range(1, count + 1)]
    largest = most if full else min(most, max(-(-total // count), total * weights[0] // sum(weights)))
    least = 1 if total - largest >= count - 1 else 0
    counts, spare = [largest] + [least] * (count - 1), total - largest - least * (count - 1)
    while spare > 0:
        candidates = [i for i in range(1, count) if counts[i] < largest] or [i for i in range(1, count) if counts[i] < most]
        mass, remaining = sum([weights[i] for i in candidates]), spare
        for i in candidates:
            extra = min(most - counts[i], max(1, remaining * weights[i] // mass), spare)
            counts[i] = counts[i] + extra
            spare = spare - extra
    return np.array(counts)


def gaussian(rng, dims, spread, most, pieces=(), kind=jnp.bfloat16):
    factor_of = shard_levels(rng, dims, pieces, -0.22, 0.18) if pieces else 1.0
    array = jax.random.normal(rng, dims, jnp.float32) * spread * factor_of
    return jnp.minimum(jnp.maximum(array, -most), most).astype(kind)


def setup_inputs(seed: int = 0) -> dict:
    arg_keys = jax.random.split(jax.random.key(seed), 6)
    wave = gaussian(arg_keys[0], (NB, BS, BS), 1.0, 6.0, ((0, 16),))
    left_env = gaussian(arg_keys[1], (W, KL, BS, BS), BS ** -0.5, 0.5, ((0, 2), (1, 16)))
    right_env = gaussian(arg_keys[2], (W, KL, BS, BS), (BS * W) ** -0.5, 0.375, ((0, 2), (1, 16)))
    right_sector_keys = jax.random.split(jax.random.fold_in(arg_keys[3], 1), NB // BLK_DEV)
    right_sector_turns = jax.random.permutation(jax.random.fold_in(arg_keys[3], 3), NB // BLK_DEV)
    right_sector = jax.vmap(lambda own, number: assign_block(jax.random.fold_in(arg_keys[3], 2), own, number, BLK_DEV, KL, 1, CAP, 2))(right_sector_keys, right_sector_turns).reshape((NB, 1))
    right_home = jax.random.permutation(arg_keys[4], KL).astype(jnp.int32)
    return dict(wave=wave, left_env=left_env, right_env=right_env, right_sector=right_sector, right_home=right_home)


def reference(wave, left_env, right_env, right_sector, right_home):
    index = jnp.arange(NB, dtype=jnp.int32)
    left_sector = (index * KL // NB).astype(jnp.int32)
    places = jnp.take(right_home, right_sector[:, 0], axis=0).astype(jnp.int32)

    def one_block(items):
        block, lsec, place = items
        lefts = jnp.take(left_env, lsec, axis=1).astype(jnp.float32)
        rights = jnp.take(right_env, place, axis=1).astype(jnp.float32)
        left = jnp.einsum("wik,kj->wij", lefts, block.astype(jnp.float32)).astype(jnp.bfloat16)
        term = jnp.einsum("wik,wjk->wij", left.astype(jnp.float32), rights)
        return jnp.sum(term, axis=0).astype(jnp.bfloat16)

    return lax.map(one_block, (wave, left_sector, places))
```

```python
import functools

import jax
import jax.numpy as jnp
from jax import lax
from jax.experimental import pallas as pl
from jax.experimental.pallas import tpu as pltpu
from jax.sharding import PartitionSpec as P

MESH = pl.DeviceIdType.MESH
PIECES = 4


def kernel(
    sizes, sector, home, wave, lenv, renv, out,
    rights, lefts, blocks_in, left, result,
    wave_sem, own_sem, x_send, x_recv, l_send, l_recv, z_send, y_send, c_send, recv, out_sem,
):
    lines, terms, chunks = sizes
    count, rows, cols = blocks_in.shape
    held, part = rights.shape[2], rights.shape[3]
    per = terms // chunks
    piece = count // PIECES
    b, m = lax.axis_index("blk"), lax.axis_index("mpo")
    z, y, c = b // 4, (b // 2) % 2, b % 2

    def at(zz, yy, cc):
        return zz * 4 + yy * 2 + cc

    sibling, across = at(z, y, 1 - c), at(z, 1 - y, c)
    peers = [lax.rem(m + d, terms) for d in range(1, terms)]

    def rows_of(term):
        return renv.at[0, :, pl.ds(pl.multiple_of(term * part, part), part), :]

    own_right = pltpu.make_async_copy(rows_of(m), rights.at[b, m], own_sem.at[0])
    own_left = pltpu.make_async_copy(lenv.at[0], lefts.at[:, m], own_sem.at[1])
    loads = [
        pltpu.make_async_copy(
            wave.at[pl.ds(i * piece, piece)], blocks_in.at[pl.ds(i * piece, piece)], wave_sem.at[i]
        )
        for i in range(PIECES)
    ]
    own_right.start()

    barrier = pltpu.get_barrier_semaphore()

    def greet(**where):
        pl.semaphore_signal(barrier, inc=1, device_id=where, device_id_type=MESH)

    for peer in peers:
        greet(mpo=peer)
    greet(blk=across)
    greet(blk=sibling)

    @pl.when(z > 0)
    def _():
        greet(blk=b - 4)

    @pl.when(z < lines - 1)
    def _():
        greet(blk=b + 4)

    own_left.start()
    for load in loads:
        load.start()
    least = jnp.where(z > 0, 1, 0) + jnp.where(z < lines - 1, 1, 0)
    pl.semaphore_wait(barrier, least + 2 + len(peers))

    x_copies = [
        pltpu.make_async_remote_copy(
            rows_of(peer), rights.at[b, m], x_send.at[i], x_recv.at[m],
            device_id={"mpo": peer}, device_id_type=MESH,
        )
        for i, peer in enumerate(peers)
    ]
    l_copies = [
        pltpu.make_async_remote_copy(
            lenv.at[0], lefts.at[:, m], l_send.at[i], l_recv.at[m],
            device_id={"mpo": peer}, device_id_type=MESH,
        )
        for i, peer in enumerate(peers)
    ]
    for copy in x_copies:
        copy.start()
    for copy in l_copies:
        copy.start()

    def unit(bb, q):
        return rights.at[bb, pl.ds(q * per, per)]

    def to(bb, q, sem, target):
        return pltpu.make_async_remote_copy(
            unit(bb, q), unit(bb, q), sem, recv.at[bb, q],
            device_id={"blk": target}, device_id_type=MESH,
        )

    def up(zz, q):
        return to(at(zz, y, c), q, z_send.at[0, zz, q], b + 4)

    def down(zz, q):
        return to(at(zz, y, c), q, z_send.at[1, zz, q], b - 4)

    def over(zz, q):
        return to(at(zz, y, c), q, y_send.at[zz, q], across)

    def beside(bb, q):
        return to(bb, q, c_send.at[bb, q], sibling)

    def spread(zz, q, upward, downward):
        if upward:

            @pl.when(z < lines - 1)
            def _():
                up(zz, q).start()

        if downward:

            @pl.when(z > 0)
            def _():
                down(zz, q).start()

        over(zz, q).start()
        beside(at(zz, y, c), q).start()

    order = [m, 1 - m] if chunks == 2 else [0]

    def wait_x(peer):
        pltpu.make_async_copy(rows_of(peer), rights.at[b, peer], x_recv.at[peer]).wait()

    def own_line():
        own_right.wait()
        if chunks == 2:
            spread(z, m, True, True)
        for peer in peers:
            wait_x(peer)
        if chunks == 2:
            spread(z, 1 - m, True, True)
        else:
            spread(z, 0, True, True)

    def hop(h):
        for q in order:

            @pl.when(z >= h)
            def _():
                beside(at(z - h, y, c), q).wait_recv()
                spread(z - h, q, True, False)

            @pl.when(z + h < lines)
            def _():
                beside(at(z + h, y, c), q).wait_recv()
                spread(z + h, q, False, True)

    def cross(h):
        for q in order:

            @pl.when(z >= h)
            def _():
                bb = at(z - h, 1 - y, c)
                beside(bb, q).wait_recv()
                beside(bb, q).start()

            if h > 0:

                @pl.when(z + h < lines)
                def _():
                    bb = at(z + h, 1 - y, c)
                    beside(bb, q).wait_recv()
                    beside(bb, q).start()

    def first(i):
        loads[i].wait()

        def body(t, carry):
            j = i * piece + 2 * t
            a = j * held // count
            stack = jnp.concatenate([lefts[a, w] for w in range(terms)], axis=0)
            pair = jnp.concatenate([blocks_in[j], blocks_in[j + 1]], axis=1)
            both = jnp.dot(stack, pair, preferred_element_type=jnp.float32).astype(jnp.bfloat16)
            for w in range(terms):
                left[j, w] = both[w * rows:(w + 1) * rows, :cols]
                left[j + 1, w] = both[w * rows:(w + 1) * rows, cols:]
            return carry

        lax.fori_loop(0, piece // 2, body, 0)

    own_line()
    own_left.wait()
    for peer in peers:
        pltpu.make_async_copy(lenv.at[0], lefts.at[:, peer], l_recv.at[peer]).wait()
    first(0)
    for h in range(1, lines):
        hop(h)
        cross(h - 1)
        if h < PIECES - 1:
            first(h)
    cross(lines - 1)
    for i in range(min(lines, PIECES - 1), PIECES):
        first(i)

    def each(body):
        def step(zz, carry):
            for q in range(chunks):
                body(zz, q)
            return carry

        lax.fori_loop(0, lines, step, 0)

    def arrived(zz, q):
        for yy in range(2):
            beside(at(zz, yy, 1 - c), q).wait_recv()

    each(arrived)

    stores = []
    for i in range(PIECES):

        def second(j, carry):
            place = home[sector[j, 0]]
            source, slot = place // held, place % held
            mine = jnp.concatenate([left[j, w] for w in range(terms)], axis=1)
            right = jnp.concatenate([rights[source, w, slot] for w in range(terms)], axis=1)
            result[j] = lax.dot_general(
                mine, right, (((1,), (1,)), ((), ())), preferred_element_type=jnp.float32
            ).astype(jnp.bfloat16)
            return carry

        lax.fori_loop(i * piece, (i + 1) * piece, second, 0, unroll=4)
        store = pltpu.make_async_copy(
            result.at[pl.ds(i * piece, piece)], out.at[pl.ds(i * piece, piece)], out_sem.at[i]
        )
        store.start()
        stores.append(store)

    for copy in x_copies:
        copy.wait_send()
    for copy in l_copies:
        copy.wait_send()

    def sent(zz, q):
        @pl.when((zz <= z) & (z < lines - 1))
        def _():
            up(zz, q).wait_send()

        @pl.when((zz >= z) & (z > 0))
        def _():
            down(zz, q).wait_send()

        over(zz, q).wait_send()
        for yy in range(2):
            beside(at(zz, yy, c), q).wait_send()

    each(sent)
    for store in stores:
        store.wait()


def local(groups, terms, wave, left_env, right_env, right_sector, right_home):
    count, rows, cols = wave.shape
    held = left_env.shape[1]
    part = rows // terms
    lines = groups // 4
    chunks = 2 if terms == 2 else 1
    bf16 = jnp.bfloat16
    dma = pltpu.SemaphoreType.DMA
    any_spec = pl.BlockSpec(memory_space=pl.ANY)
    smem = pl.BlockSpec(memory_space=pltpu.SMEM)
    need = 2 * (
        groups * terms * held * part * cols + held * terms * rows * cols
        + count * rows * cols * (2 + terms)
    )
    return pl.pallas_call(
        functools.partial(kernel, (lines, terms, chunks)),
        out_shape=jax.ShapeDtypeStruct((count, rows, part), bf16),
        in_specs=[smem, smem, any_spec, any_spec, any_spec],
        out_specs=any_spec,
        scratch_shapes=[
            pltpu.VMEM((groups, terms, held, part, cols), bf16),
            pltpu.VMEM((held, terms, rows, cols), bf16),
            pltpu.VMEM((count, rows, cols), bf16),
            pltpu.VMEM((count, terms, rows, cols), bf16),
            pltpu.VMEM((count, rows, part), bf16),
            dma((PIECES,)),
            dma((2,)),
            dma((terms,)),
            dma((terms,)),
            dma((terms,)),
            dma((terms,)),
            dma((2, lines, chunks)),
            dma((lines, chunks)),
            dma((groups, chunks)),
            dma((groups, chunks)),
            dma((PIECES,)),
        ],
        compiler_params=pltpu.CompilerParams(
            collective_id=0, has_side_effects=True, vmem_limit_bytes=need + (8 << 20)
        ),
        cost_estimate=pl.CostEstimate(
            flops=4 * count * terms * rows * rows * cols,
            bytes_accessed=2 * count * rows * (cols + part),
            transcendentals=0,
        ),
    )(right_sector, right_home, wave, left_env, right_env)


def solution(mesh):
    groups, terms = mesh.shape["blk"], mesh.shape["mpo"]
    in_specs = (
        P("blk", None, None),
        P("mpo", "blk", None, None),
        P("mpo", "blk", None, None),
        P("blk", None),
        P(),
    )
    return jax.shard_map(
        functools.partial(local, groups, terms),
        mesh=mesh,
        in_specs=in_specs,
        out_specs=P("blk", None, "mpo"),
        check_vma=False,
    )
```

```python
import functools

import jax
import jax.numpy as jnp
from jax import lax
from jax.experimental import pallas as pl
from jax.experimental.pallas import tpu as pltpu
from jax.sharding import PartitionSpec as P

MESH = pl.DeviceIdType.MESH
PIECES = 8


def kernel(
    sizes, sector, home, wave, lenv, renv, out,
    rights, lefts, blocks_in, left, result,
    wave_sem, own_sem, x_send, x_recv, l_send, l_recv, z_send, y_send, c_send, recv, out_sem,
):
    lines, terms, chunks = sizes
    count, rows, cols = blocks_in.shape
    held, part = rights.shape[2], rights.shape[3]
    per = terms // chunks
    piece = count // PIECES
    b, m = lax.axis_index("blk"), lax.axis_index("mpo")
    z, y, c = b // 4, (b // 2) % 2, b % 2

    def at(zz, yy, cc):
        return zz * 4 + yy * 2 + cc

    sibling, across = at(z, y, 1 - c), at(z, 1 - y, c)
    peers = [lax.rem(m + d, terms) for d in range(1, terms)]

    def rows_of(term):
        return renv.at[0, :, pl.ds(pl.multiple_of(term * part, part), part), :]

    own_right = pltpu.make_async_copy(rows_of(m), rights.at[b, m], own_sem.at[0])
    own_left = pltpu.make_async_copy(lenv.at[0], lefts.at[:, m], own_sem.at[1])
    loads = [
        pltpu.make_async_copy(
            wave.at[pl.ds(i * piece, piece)], blocks_in.at[pl.ds(i * piece, piece)], wave_sem.at[i]
        )
        for i in range(PIECES)
    ]
    own_right.start()

    barrier = pltpu.get_barrier_semaphore()

    def greet(**where):
        pl.semaphore_signal(barrier, inc=1, device_id=where, device_id_type=MESH)

    for peer in peers:
        greet(mpo=peer)
    greet(blk=across)
    greet(blk=sibling)

    @pl.when(z > 0)
    def _():
        greet(blk=b - 4)

    @pl.when(z < lines - 1)
    def _():
        greet(blk=b + 4)

    own_left.start()
    for load in loads:
        load.start()
    least = jnp.where(z > 0, 1, 0) + jnp.where(z < lines - 1, 1, 0)
    pl.semaphore_wait(barrier, least + 2 + len(peers))

    x_copies = [
        pltpu.make_async_remote_copy(
            rows_of(peer), rights.at[b, m], x_send.at[i], x_recv.at[m],
            device_id={"mpo": peer}, device_id_type=MESH,
        )
        for i, peer in enumerate(peers)
    ]
    l_copies = [
        pltpu.make_async_remote_copy(
            lenv.at[0], lefts.at[:, m], l_send.at[i], l_recv.at[m],
            device_id={"mpo": peer}, device_id_type=MESH,
        )
        for i, peer in enumerate(peers)
    ]
    for copy in x_copies:
        copy.start()
    for copy in l_copies:
        copy.start()

    def unit(bb, q):
        return rights.at[bb, pl.ds(q * per, per)]

    def to(bb, q, sem, target):
        return pltpu.make_async_remote_copy(
            unit(bb, q), unit(bb, q), sem, recv.at[bb, q],
            device_id={"blk": target}, device_id_type=MESH,
        )

    def up(zz, q):
        return to(at(zz, y, c), q, z_send.at[0, zz, q], b + 4)

    def down(zz, q):
        return to(at(zz, y, c), q, z_send.at[1, zz, q], b - 4)

    def over(zz, q):
        return to(at(zz, y, c), q, y_send.at[zz, q], across)

    def beside(bb, q):
        return to(bb, q, c_send.at[bb, q], sibling)

    def spread(zz, q, upward, downward):
        if upward:

            @pl.when(z < lines - 1)
            def _():
                up(zz, q).start()

        if downward:

            @pl.when(z > 0)
            def _():
                down(zz, q).start()

        over(zz, q).start()
        beside(at(zz, y, c), q).start()

    order = [m, 1 - m] if chunks == 2 else [0]

    def wait_x(peer):
        pltpu.make_async_copy(rows_of(peer), rights.at[b, peer], x_recv.at[peer]).wait()

    def own_line():
        own_right.wait()
        if chunks == 2:
            spread(z, m, True, True)
        for peer in peers:
            wait_x(peer)
        if chunks == 2:
            spread(z, 1 - m, True, True)
        else:
            spread(z, 0, True, True)

    def hop(h):
        for q in order:

            @pl.when(z >= h)
            def _():
                beside(at(z - h, y, c), q).wait_recv()
                spread(z - h, q, True, False)

            @pl.when(z + h < lines)
            def _():
                beside(at(z + h, y, c), q).wait_recv()
                spread(z + h, q, False, True)

    def cross(h):
        for q in order:

            @pl.when(z >= h)
            def _():
                bb = at(z - h, 1 - y, c)
                beside(bb, q).wait_recv()
                beside(bb, q).start()

            if h > 0:

                @pl.when(z + h < lines)
                def _():
                    bb = at(z + h, 1 - y, c)
                    beside(bb, q).wait_recv()
                    beside(bb, q).start()

    def first(i):
        loads[i].wait()

        def body(t, carry):
            j = i * piece + 2 * t
            a = j * held // count
            pair = jnp.concatenate([blocks_in[j], blocks_in[j + 1]], axis=1)
            for w in range(terms):
                both = jnp.dot(lefts[a, w], pair, preferred_element_type=jnp.float32).astype(jnp.bfloat16)
                left[j, w] = both[:, :cols]
                left[j + 1, w] = both[:, cols:]
            return carry

        lax.fori_loop(0, piece // 2, body, 0, unroll=6)

    own_line()
    hop(1)
    own_left.wait()
    for peer in peers:
        pltpu.make_async_copy(lenv.at[0], lefts.at[:, peer], l_recv.at[peer]).wait()
    done = 0
    for h in range(2, lines):
        if done < PIECES:
            first(done)
            done += 1
        hop(h)
    for h in range(lines):
        if done < PIECES:
            first(done)
            done += 1
        cross(h)
    for i in range(done, PIECES):
        first(i)

    def each(body):
        def step(zz, carry):
            for q in range(chunks):
                body(zz, q)
            return carry

        lax.fori_loop(0, lines, step, 0)

    def arrived(zz, q):
        for yy in range(2):
            beside(at(zz, yy, 1 - c), q).wait_recv()

    each(arrived)

    stores = []
    for i in range(PIECES):

        def second(j, carry):
            place = home[sector[0, j]]
            source, slot = place // held, place % held
            mine = jnp.concatenate([left[j, w] for w in range(terms)], axis=1)
            right = jnp.concatenate([rights[source, w, slot] for w in range(terms)], axis=1)
            result[j] = lax.dot_general(
                right, mine, (((1,), (1,)), ((), ())), preferred_element_type=jnp.float32
            ).astype(jnp.bfloat16)
            return carry

        lax.fori_loop(i * piece, (i + 1) * piece, second, 0, unroll=12)
        store = pltpu.make_async_copy(
            result.at[pl.ds(i * piece, piece)], out.at[pl.ds(i * piece, piece)], out_sem.at[i]
        )
        store.start()
        stores.append(store)

    for copy in x_copies:
        copy.wait_send()
    for copy in l_copies:
        copy.wait_send()

    def sent(zz, q):
        @pl.when((zz <= z) & (z < lines - 1))
        def _():
            up(zz, q).wait_send()

        @pl.when((zz >= z) & (z > 0))
        def _():
            down(zz, q).wait_send()

        over(zz, q).wait_send()
        for yy in range(2):
            beside(at(zz, yy, c), q).wait_send()

    each(sent)
    for store in stores:
        store.wait()


def local(groups, terms, wave, left_env, right_env, right_sector, right_home):
    count, rows, cols = wave.shape
    held = left_env.shape[1]
    part = rows // terms
    lines = groups // 4
    chunks = 2 if terms == 2 else 1
    bf16 = jnp.bfloat16
    dma = pltpu.SemaphoreType.DMA
    any_spec = pl.BlockSpec(memory_space=pl.ANY)
    smem = pl.BlockSpec(memory_space=pltpu.SMEM)
    product = pl.pallas_call(
        functools.partial(kernel, (lines, terms, chunks)),
        out_shape=jax.ShapeDtypeStruct((count, part, rows), bf16),
        in_specs=[smem, smem, any_spec, any_spec, any_spec],
        out_specs=any_spec,
        scratch_shapes=[
            pltpu.VMEM((groups, terms, held, part, cols), bf16),
            pltpu.VMEM((held, terms, rows, cols), bf16),
            pltpu.VMEM((count, rows, cols), bf16),
            pltpu.VMEM((count, terms, rows, cols), bf16),
            pltpu.VMEM((count, part, rows), bf16),
            dma((PIECES,)),
            dma((2,)),
            dma((terms,)),
            dma((terms,)),
            dma((terms,)),
            dma((terms,)),
            dma((2, lines, chunks)),
            dma((lines, chunks)),
            dma((groups, chunks)),
            dma((groups, chunks)),
            dma((PIECES,)),
        ],
        compiler_params=pltpu.CompilerParams(
            collective_id=0, has_side_effects=True, vmem_limit_bytes=60 << 20
        ),
        cost_estimate=pl.CostEstimate(
            flops=4 * count * terms * rows * rows * cols,
            bytes_accessed=2 * count * rows * (cols + part),
            transcendentals=0,
        ),
    )(right_sector.reshape(1, count), right_home, wave, left_env, right_env)
    return jnp.swapaxes(product, 1, 2)


def solution(mesh):
    groups, terms = mesh.shape["blk"], mesh.shape["mpo"]
    in_specs = (
        P("blk", None, None),
        P("mpo", "blk", None, None),
        P("mpo", "blk", None, None),
        P("blk", None),
        P(),
    )
    return jax.shard_map(
        functools.partial(local, groups, terms),
        mesh=mesh,
        in_specs=in_specs,
        out_specs=P("blk", None, "mpo"),
        check_vma=False,
    )
```

```python
import functools

import jax
import jax.numpy as jnp
from jax import lax
from jax.experimental import pallas as pl
from jax.experimental.pallas import tpu as pltpu
from jax.sharding import PartitionSpec as P

MESH = pl.DeviceIdType.MESH
PIECES = 8


def kernel(
    sizes, sector, home, wave, lenv, renv, out,
    rights, lefts, blocks_in, left, result,
    wave_sem, own_sem, x_send, x_recv, l_send, l_recv, z_send, y_send, c_send, recv, out_sem,
):
    lines, terms, chunks = sizes
    count, rows, cols = blocks_in.shape
    held, part = rights.shape[2], rights.shape[3]
    per = terms // chunks
    piece = count // PIECES
    b, m = lax.axis_index("blk"), lax.axis_index("mpo")
    z, y, c = b // 4, (b // 2) % 2, b % 2

    def at(zz, yy, cc):
        return zz * 4 + yy * 2 + cc

    sibling, across = at(z, y, 1 - c), at(z, 1 - y, c)
    peers = [lax.rem(m + d, terms) for d in range(1, terms)]

    def rows_of(term):
        return renv.at[0, :, pl.ds(pl.multiple_of(term * part, part), part), :]

    own_right = pltpu.make_async_copy(rows_of(m), rights.at[b, m], own_sem.at[0])
    own_left = pltpu.make_async_copy(lenv.at[0], lefts.at[:, m], own_sem.at[1])
    loads = [
        pltpu.make_async_copy(
            wave.at[pl.ds(i * piece, piece)], blocks_in.at[pl.ds(i * piece, piece)], wave_sem.at[i]
        )
        for i in range(PIECES)
    ]
    own_right.start()

    barrier = pltpu.get_barrier_semaphore()

    def greet(**where):
        pl.semaphore_signal(barrier, inc=1, device_id=where, device_id_type=MESH)

    for peer in peers:
        greet(mpo=peer)
    greet(blk=across)
    greet(blk=sibling)

    @pl.when(z > 0)
    def _():
        greet(blk=b - 4)

    @pl.when(z < lines - 1)
    def _():
        greet(blk=b + 4)

    own_left.start()
    for load in loads:
        load.start()
    least = jnp.where(z > 0, 1, 0) + jnp.where(z < lines - 1, 1, 0)
    pl.semaphore_wait(barrier, least + 2 + len(peers))

    x_copies = [
        pltpu.make_async_remote_copy(
            rows_of(peer), rights.at[b, m], x_send.at[i], x_recv.at[m],
            device_id={"mpo": peer}, device_id_type=MESH,
        )
        for i, peer in enumerate(peers)
    ]
    l_copies = [
        pltpu.make_async_remote_copy(
            lenv.at[0], lefts.at[:, m], l_send.at[i], l_recv.at[m],
            device_id={"mpo": peer}, device_id_type=MESH,
        )
        for i, peer in enumerate(peers)
    ]
    for copy in x_copies:
        copy.start()

    def unit(bb, q):
        return rights.at[bb, pl.ds(q * per, per)]

    def to(bb, q, sem, target):
        return pltpu.make_async_remote_copy(
            unit(bb, q), unit(bb, q), sem, recv.at[bb, q],
            device_id={"blk": target}, device_id_type=MESH,
        )

    def up(zz, q):
        return to(at(zz, y, c), q, z_send.at[0, zz, q], b + 4)

    def down(zz, q):
        return to(at(zz, y, c), q, z_send.at[1, zz, q], b - 4)

    def over(zz, q):
        return to(at(zz, y, c), q, y_send.at[zz, q], across)

    def beside(bb, q):
        return to(bb, q, c_send.at[bb, q], sibling)

    def spread(zz, q, upward, downward):
        over(zz, q).start()
        if upward:

            @pl.when(z < lines - 1)
            def _():
                up(zz, q).start()

        if downward:

            @pl.when(z > 0)
            def _():
                down(zz, q).start()

        beside(at(zz, y, c), q).start()

    order = [m, 1 - m] if chunks == 2 else [0]

    def wait_x(peer):
        pltpu.make_async_copy(rows_of(peer), rights.at[b, peer], x_recv.at[peer]).wait()

    def own_line():
        own_right.wait()
        if chunks == 2:
            spread(z, m, True, True)
        for peer in peers:
            wait_x(peer)
        if chunks == 2:
            spread(z, 1 - m, True, True)
        else:
            spread(z, 0, True, True)

    def hop(h):
        for q in order:

            @pl.when(z >= h)
            def _():
                beside(at(z - h, y, c), q).wait_recv()
                spread(z - h, q, True, False)

            @pl.when(z + h < lines)
            def _():
                beside(at(z + h, y, c), q).wait_recv()
                spread(z + h, q, False, True)

    def cross(h):
        for q in order:

            @pl.when(z >= h)
            def _():
                bb = at(z - h, 1 - y, c)
                beside(bb, q).wait_recv()
                beside(bb, q).start()

            if h > 0:

                @pl.when(z + h < lines)
                def _():
                    bb = at(z + h, 1 - y, c)
                    beside(bb, q).wait_recv()
                    beside(bb, q).start()

    def first(i):
        loads[i].wait()

        def body(t, carry):
            j = i * piece + 2 * t
            a = j * held // count
            pair = jnp.concatenate([blocks_in[j], blocks_in[j + 1]], axis=1)
            for w in range(terms):
                both = jnp.dot(lefts[a, w], pair, preferred_element_type=jnp.float32).astype(jnp.bfloat16)
                left[j, w] = both[:, :cols]
                left[j + 1, w] = both[:, cols:]
            return carry

        lax.fori_loop(0, piece // 2, body, 0, unroll=6)

    own_line()
    for copy in l_copies:
        copy.start()
    hop(1)
    own_left.wait()
    for peer in peers:
        pltpu.make_async_copy(lenv.at[0], lefts.at[:, peer], l_recv.at[peer]).wait()
    done = 0
    for h in range(2, lines):
        if done < PIECES:
            first(done)
            done += 1
        hop(h)
    for h in range(lines):
        if done < PIECES:
            first(done)
            done += 1
        cross(h)
    for i in range(done, PIECES):
        first(i)

    def each(body):
        def step(zz, carry):
            for q in range(chunks):
                body(zz, q)
            return carry

        lax.fori_loop(0, lines, step, 0)

    def arrived(zz, q):
        for yy in range(2):
            beside(at(zz, yy, 1 - c), q).wait_recv()

    each(arrived)

    stores = []
    for i in range(PIECES):

        def second(j, carry):
            place = home[sector[0, j]]
            source, slot = place // held, place % held
            mine = jnp.concatenate([left[j, w] for w in range(terms)], axis=1)
            right = jnp.concatenate([rights[source, w, slot] for w in range(terms)], axis=1)
            result[j] = lax.dot_general(
                right, mine, (((1,), (1,)), ((), ())), preferred_element_type=jnp.float32
            ).astype(jnp.bfloat16)
            return carry

        lax.fori_loop(i * piece, (i + 1) * piece, second, 0, unroll=12)
        store = pltpu.make_async_copy(
            result.at[pl.ds(i * piece, piece)], out.at[pl.ds(i * piece, piece)], out_sem.at[i]
        )
        store.start()
        stores.append(store)

    for copy in x_copies:
        copy.wait_send()
    for copy in l_copies:
        copy.wait_send()

    def sent(zz, q):
        @pl.when((zz <= z) & (z < lines - 1))
        def _():
            up(zz, q).wait_send()

        @pl.when((zz >= z) & (z > 0))
        def _():
            down(zz, q).wait_send()

        over(zz, q).wait_send()
        for yy in range(2):
            beside(at(zz, yy, c), q).wait_send()

    each(sent)
    for store in stores:
        store.wait()


def local(groups, terms, wave, left_env, right_env, right_sector, right_home):
    count, rows, cols = wave.shape
    held = left_env.shape[1]
    part = rows // terms
    lines = groups // 4
    chunks = 2 if terms == 2 else 1
    bf16 = jnp.bfloat16
    dma = pltpu.SemaphoreType.DMA
    any_spec = pl.BlockSpec(memory_space=pl.ANY)
    smem = pl.BlockSpec(memory_space=pltpu.SMEM)
    product = pl.pallas_call(
        functools.partial(kernel, (lines, terms, chunks)),
        out_shape=jax.ShapeDtypeStruct((count, part, rows), bf16),
        in_specs=[smem, smem, any_spec, any_spec, any_spec],
        out_specs=any_spec,
        scratch_shapes=[
            pltpu.VMEM((groups, terms, held, part, cols), bf16),
            pltpu.VMEM((held, terms, rows, cols), bf16),
            pltpu.VMEM((count, rows, cols), bf16),
            pltpu.VMEM((count, terms, rows, cols), bf16),
            pltpu.VMEM((count, part, rows), bf16),
            dma((PIECES,)),
            dma((2,)),
            dma((terms,)),
            dma((terms,)),
            dma((terms,)),
            dma((terms,)),
            dma((2, lines, chunks)),
            dma((lines, chunks)),
            dma((groups, chunks)),
            dma((groups, chunks)),
            dma((PIECES,)),
        ],
        compiler_params=pltpu.CompilerParams(
            collective_id=0, has_side_effects=True, vmem_limit_bytes=60 << 20
        ),
        cost_estimate=pl.CostEstimate(
            flops=4 * count * terms * rows * rows * cols,
            bytes_accessed=2 * count * rows * (cols + part),
            transcendentals=0,
        ),
    )(right_sector.reshape(1, count), right_home, wave, left_env, right_env)
    return jnp.swapaxes(product, 1, 2)


def solution(mesh):
    groups, terms = mesh.shape["blk"], mesh.shape["mpo"]
    in_specs = (
        P("blk", None, None),
        P("mpo", "blk", None, None),
        P("mpo", "blk", None, None),
        P("blk", None),
        P(),
    )
    return jax.shard_map(
        functools.partial(local, groups, terms),
        mesh=mesh,
        in_specs=in_specs,
        out_specs=P("blk", None, "mpo"),
        check_vma=False,
    )
```
